32 devices in a mesh: stretch: 8 (over z, y), head: 2 (over x), cfg: 2 (over core).
Axes of the slice: x: 2, y: 2, z: 4, core: 2. Of those that a mesh axis runs over, the one named last changes fastest.
Arguments:
- queries: bfloat16 [14336, 5120], P(('cfg', 'stretch', 'head')), parts along dimension 0, may hold values from -6 to 6
- keys: bfloat16 [14336, 5120], P(('cfg', 'stretch', 'head')), parts along dimension 0, may hold values from -6 to 6
- values: bfloat16 [14336, 5120], P(('cfg', 'stretch', 'head')), parts along dimension 0, may hold values from -6 to 6
- frames: int32 [8], replicated, may hold values from 4 to 7, as said below
- motion: int32 [8], replicated, may hold values from 0 to 4, as said below
Outputs:
- attended: bfloat16 [14336, 5120], P(('cfg', 'stretch', 'head')), parts along dimension 0
The draws below stay inside these ranges and needn't reach their ends.
There are 2 independent parts, one for each index of `cfg`. The reference program is written for one: setup_inputs(seed, part) draws one part's arguments, and reference() takes and returns one part's arrays. A program takes and returns all parts, laid end to end along the dimension named above; an argument that names none is the same for every part. Nothing has to cross between parts.
Inputs may be any that keep to these rules, and one draw needn't show every extreme that they name: Every stretch holds at least 4 frames; some stretch holds 7. `motion`: stretch 0 takes none; some stretch takes 4.
All inputs are finite; a program needn't handle non-finite values.
Results may differ from the reference program's by a relative error of at most 0.0046.
Values may be sent and summed in bfloat16 or wider, within the bound.
A program may use at most 128 MiB of HBM per device.

```python
import math
import jax
import jax.numpy as jnp
from jax import lax

HEADS = 40
HD = 128
FT = 128
FRAMES = 7
MOT_CAP = 4
STRETCHES = 8
TOKENS = 7168


def base_field(key, salt):
    inner = jax.random.fold_in(key, salt)
    raw = jax.random.normal(jax.random.fold_in(inner, 1), (TOKENS, HEADS * HD), jnp.float32)
    return raw


def draw_queries(key, part):
    field = base_field(key, 3)
    return jnp.clip(field, -6.0, 6.0).astype(jnp.bfloat16)


def draw_keys(key, part):
    field = base_field(key, 4)
    return jnp.clip(field, -6.0, 6.0).astype(jnp.bfloat16)


def draw_values(key, part):
    field = base_field(key, 5)
    return jnp.clip(field, -6.0, 6.0).astype(jnp.bfloat16)


def draw_frames(key, part):
    counts = jax.random.randint(jax.random.fold_in(key, 5), (STRETCHES,), MOT_CAP, FRAMES + 1)
    fullest = jax.random.randint(jax.random.fold_in(key, 6), (), 0, STRETCHES)
    return counts.at[fullest].set(FRAMES).astype(jnp.int32)


def draw_motion(key, part):
    counts = jax.random.randint(jax.random.fold_in(key, 8), (STRETCHES,), 1, MOT_CAP + 1)
    most = jax.random.randint(jax.random.fold_in(key, 9), (), 1, STRETCHES)
    counts = counts.at[most].set(MOT_CAP)
    return counts.at[0].set(0).astype(jnp.int32)


def setup_inputs(seed: int = 0, part: int = 0) -> dict:
    splits = jax.random.split(jax.random.key(seed), 6)
    part_splits = jax.random.split(jax.random.fold_in(splits[5], part), 6)
    queries = draw_queries(jax.random.fold_in(jax.random.fold_in(splits[5], part), 71), part)
    keys = draw_keys(jax.random.fold_in(jax.random.fold_in(splits[5], part), 71), part)
    values = draw_values(jax.random.fold_in(jax.random.fold_in(splits[5], part), 71), part)
    frames = draw_frames(jax.random.fold_in(splits[5], 71), part)
    motion = draw_motion(jax.random.fold_in(splits[5], 71), part)
    return {"queries": queries, "keys": keys, "values": values, "frames": frames, "motion": motion}


NEG = -1e+30

def head_block(q_head, k_head, v_head, key_live):
    scores = lax.dot_general(q_head, k_head, (((1,), (1,)), ((), ())), preferred_element_type=jnp.float32)
    scores = scores * (1.0 / math.sqrt(q_head.shape[1]))
    masked = jnp.where(key_live[None, :], scores, NEG)
    top = lax.optimization_barrier(jnp.max(masked, axis=1))
    weights = jnp.where(key_live[None, :], jnp.exp(masked - top[:, None]), 0.0)
    total = lax.optimization_barrier(jnp.sum(weights, axis=1))
    acc = jnp.dot(weights.astype(jnp.bfloat16), v_head, preferred_element_type=jnp.float32)
    return (top, total, acc)

def pick_head(array, index):
    return lax.dynamic_index_in_dim(array, index, 1, keepdims=False)

def own_part(queries, keys, values, key_live):
    rows, count, width = queries.shape
    start = (jnp.zeros((rows, count), jnp.float32), jnp.zeros((rows, count), jnp.float32), jnp.zeros((rows, count, width), jnp.float32))

    def step(index, carry):
        tops, totals, accs = carry
        top, total, acc = head_block(pick_head(queries, index), pick_head(keys, index), pick_head(values, index), key_live)
        tops = lax.dynamic_update_index_in_dim(tops, top, index, 1)
        totals = lax.dynamic_update_index_in_dim(totals, total, index, 1)
        accs = lax.dynamic_update_index_in_dim(accs, acc, index, 1)
        return (tops, totals, accs)
    return lax.fori_loop(0, count, step, start)

def finish(queries, motion_keys, motion_values, motion_live, query_live, partial_value):
    tops, totals, accs = partial_value
    count = queries.shape[1]

    def step(index, result):
        top, total, acc = head_block(pick_head(queries, index), pick_head(motion_keys, index), pick_head(motion_values, index), motion_live)
        top_own = pick_head(tops, index)
        total_own = pick_head(totals, index)
        acc_own = pick_head(accs, index)
        peak = jnp.maximum(top_own, top)
        factor_own = jnp.exp(top_own - peak)
        factor_mot = jnp.exp(top - peak)
        mixed = (acc_own * factor_own[:, None] + acc * factor_mot[:, None]) / (total_own * factor_own + total * factor_mot)[:, None]
        mixed = jnp.where(query_live[:, None], mixed, 0.0).astype(jnp.bfloat16)
        return lax.dynamic_update_index_in_dim(result, mixed, index, 1)
    return lax.fori_loop(0, count, step, jnp.zeros(queries.shape, jnp.bfloat16))

def reference(queries, keys, values, frames, motion):
    width = queries.shape[1]
    span = FRAMES * FT
    tail = MOT_CAP * FT
    spot = jnp.arange(span, dtype=jnp.int32) // FT
    slot = jnp.arange(tail, dtype=jnp.int32) // FT

    def take(array, begin, length):
        return lax.dynamic_slice_in_dim(array, begin, length, 0).reshape(length, HEADS, HD)

    def one_stretch(index):
        begin = (index * span).astype(jnp.int32)
        prior = jnp.maximum(index - 1, 0).astype(jnp.int32)
        tail_begin = (prior * span + (frames[prior] - MOT_CAP) * FT).astype(jnp.int32)
        live = spot < frames[index]
        motion_live = slot >= MOT_CAP - motion[index]
        q_stretch = take(queries, begin, span)
        partial_value = own_part(q_stretch, take(keys, begin, span), take(values, begin, span), live)
        mixed = finish(q_stretch, take(keys, tail_begin, tail), take(values, tail_begin, tail), motion_live, live, partial_value)
        return mixed.reshape(span, width)
    blocks = lax.map(one_stretch, jnp.arange(STRETCHES, dtype=jnp.int32))
    return blocks.reshape(STRETCHES * span, width)
```

```python
import functools
import math

import jax
import jax.numpy as jnp
from jax import lax
from jax.experimental import pallas as pl
from jax.experimental.pallas import tpu as pltpu
from jax.sharding import PartitionSpec as P

HD = 128
FT = 128
FRAMES = 7
MOT_CAP = 4
NEG = -1e30
MESH = pl.DeviceIdType.MESH

AHEAD = 4
LEAD = 2


def kernel(
    groups, stretches, count, rows, sub,
    frames_ref, motion_ref, q_ref, k_ref, v_ref, out_ref,
    qb, kb, vb, kt, vt, ob, bias,
    in_send, in_recv, in_local, out_send, out_recv, out_local, mot_send, mot_recv,
):
    span = rows * groups
    tail = MOT_CAP * FT
    local = count * HD
    me = lax.axis_index("head")
    stretch = lax.axis_index("stretch")
    after = lax.rem(stretch + 1, stretches)
    before = lax.rem(stretch + stretches - 1, stretches)
    live_frames = frames_ref[stretch]
    motion_frames = motion_ref[stretch]

    def peer(offset):
        return lax.rem(me + offset, groups)

    def rows_of(owner):
        return pl.ds(pl.multiple_of(owner * rows, 16), rows)

    def columns(owner, head):
        return pl.ds(pl.multiple_of(owner * local + head * HD, HD), HD)

    sources = (k_ref, v_ref, q_ref)
    targets = (kb, vb, qb)

    def exchange(which, head, offset, owner):
        to = peer(offset)
        land = me if owner is None else owner
        return pltpu.make_async_remote_copy(
            src_ref=sources[which].at[:, columns(to, head)],
            dst_ref=targets[which].at[head, rows_of(land), :],
            send_sem=in_send.at[which, head, offset - 1],
            recv_sem=in_recv.at[which, head, offset - 1],
            device_id={"head": to},
            device_id_type=MESH,
        )

    def keep(which, head):
        return pltpu.make_async_copy(
            sources[which].at[:, columns(me, head)],
            targets[which].at[head, rows_of(me), :],
            in_local.at[which, head],
        )

    def pass_on(which, head):
        return pltpu.make_async_remote_copy(
            src_ref=(kt, vt)[which].at[head],
            dst_ref=(kb, vb)[which].at[head, pl.ds(span, tail), :],
            send_sem=mot_send.at[which, head],
            recv_sem=mot_recv.at[which, head],
            device_id={"stretch": after},
            device_id_type=MESH,
        )

    def give_back(head, offset, owner):
        to = peer(offset)
        group = me if owner is None else owner
        return pltpu.make_async_remote_copy(
            src_ref=ob.at[head, rows_of(to), :],
            dst_ref=out_ref.at[:, columns(group, head)],
            send_sem=out_send.at[head, offset - 1],
            recv_sem=out_recv.at[head, offset - 1],
            device_id={"head": to},
            device_id_type=MESH,
        )

    def own_output(head):
        return pltpu.make_async_copy(
            ob.at[head, rows_of(me), :],
            out_ref.at[:, columns(me, head)],
            out_local.at[head],
        )

    def start(which, head):
        for offset in range(1, groups):
            exchange(which, head, offset, None).start()
        keep(which, head).start()

    def arrived(which, head):
        keep(which, head).wait()
        for offset in range(1, groups):
            exchange(which, head, offset, peer(groups - offset)).wait_recv()

    def slot(index):
        @pl.when(index < count)
        def _():
            start(0, index)
            start(1, index)

        @pl.when(jnp.logical_and(index >= 1, index <= count))
        def _():
            start(2, index - 1)

    def forward(head):
        for which, (buffer, ready) in enumerate(((kb, kt), (vb, vt))):
            arrived(which, head)
            for block in range(MOT_CAP):
                chosen = buffer[head, pl.ds(block * FT, FT), :].astype(jnp.float32)
                for skip in range(1, FRAMES - MOT_CAP + 1):
                    other = buffer[head, pl.ds((block + skip) * FT, FT), :].astype(jnp.float32)
                    chosen = jnp.where(live_frames == MOT_CAP + skip, other, chosen)
                ready[head, pl.ds(block * FT, FT), :] = chosen.astype(jnp.bfloat16)
            pass_on(which, head).start()

    scale = math.log2(math.e) / math.sqrt(HD)

    def attend(head, base):
        scores = lax.dot_general(
            qb[head, pl.ds(base, sub), :], kb[head],
            (((1,), (1,)), ((), ())), preferred_element_type=jnp.float32,
        )
        scores = scores * scale + bias[...]
        top = jnp.max(scores, axis=1, keepdims=True)
        weights = jnp.exp2(scores - top)
        total = jnp.sum(weights, axis=1, keepdims=True)
        acc = jnp.dot(weights.astype(jnp.bfloat16), vb[head], preferred_element_type=jnp.float32)
        row = base + lax.broadcasted_iota(jnp.int32, (sub, 1), 0)
        mixed = jnp.where(row < live_frames * FT, acc / total, 0.0)
        ob[head, pl.ds(base, sub), :] = mixed.astype(jnp.bfloat16)

    barrier = pltpu.get_barrier_semaphore()
    for offset in range(1, groups):
        pl.semaphore_signal(barrier, inc=1, device_id={"head": peer(offset)}, device_id_type=MESH)
    for other in (after, before):
        pl.semaphore_signal(barrier, inc=1, device_id={"stretch": other}, device_id_type=MESH)
    pl.semaphore_wait(barrier, groups + 1)

    for index in range(AHEAD):
        slot(jnp.int32(index))

    spot = lax.broadcasted_iota(jnp.int32, (1, span + tail), 1)
    own = jnp.logical_and(spot < span, spot < live_frames * FT)
    mot = spot >= span + (MOT_CAP - motion_frames) * FT
    bias[...] = jnp.where(jnp.logical_or(own, mot), 0.0, NEG)

    for head in range(LEAD):
        forward(jnp.int32(head))

    def step(head, carry):
        slot(head + AHEAD)

        @pl.when(head + LEAD < count)
        def _():
            forward(head + LEAD)

        arrived(2, head)
        for which in range(2):
            pass_on(which, head).wait_recv()
        for offset in range(1, groups + 1):
            owner = peer(offset)

            def block(index, c):
                attend(head, pl.multiple_of(owner * rows + index * sub, 16))
                return c

            lax.fori_loop(0, rows // sub, block, 0)
            if offset < groups:
                give_back(head, offset, None).start()
            else:
                own_output(head).start()
        return carry

    lax.fori_loop(0, count, step, 0)

    def drain(head, carry):
        for which in range(3):
            for offset in range(1, groups):
                exchange(which, head, offset, None).wait_send()
        for which in range(2):
            pass_on(which, head).wait_send()
        for offset in range(1, groups):
            give_back(head, offset, None).wait_send()
            give_back(head, offset, peer(groups - offset)).wait_recv()
        own_output(head).wait()
        return carry

    lax.fori_loop(0, count, drain, 0)


def body(groups, stretches, queries, keys, values, frames, motion):
    rows, width = queries.shape
    span = rows * groups
    tail = MOT_CAP * FT
    local = width // groups
    count = local // HD
    sub = rows // 2 if rows > 256 else rows
    wide = jnp.bfloat16
    dma = pltpu.SemaphoreType.DMA
    return pl.pallas_call(
        functools.partial(kernel, groups, stretches, count, rows, sub),
        out_shape=jax.ShapeDtypeStruct((rows, width), wide),
        in_specs=[pl.BlockSpec(memory_space=pltpu.SMEM)] * 2
        + [pl.BlockSpec(memory_space=pltpu.HBM)] * 3,
        out_specs=pl.BlockSpec(memory_space=pltpu.HBM),
        scratch_shapes=[
            pltpu.VMEM((count, span, HD), wide),
            pltpu.VMEM((count, span + tail, HD), wide),
            pltpu.VMEM((count, span + tail, HD), wide),
            pltpu.VMEM((count, tail, HD), wide),
            pltpu.VMEM((count, tail, HD), wide),
            pltpu.VMEM((count, span, HD), wide),
            pltpu.VMEM((1, span + tail), jnp.float32),
            dma((3, count, groups - 1)),
            dma((3, count, groups - 1)),
            dma((3, count)),
            dma((count, groups - 1)),
            dma((count, groups - 1)),
            dma((count,)),
            dma((2, count)),
            dma((2, count)),
        ],
        compiler_params=pltpu.CompilerParams(
            collective_id=0, has_side_effects=True, vmem_limit_bytes=56 * 1024 * 1024
        ),
        cost_estimate=pl.CostEstimate(
            flops=4 * span * (span + tail) * local,
            bytes_accessed=8 * rows * width,
            transcendentals=span * (span + tail) * count,
        ),
    )(frames, motion, queries, keys, values)


def solution(mesh):
    placed = P(("cfg", "stretch", "head"), None)
    return jax.shard_map(
        functools.partial(body, mesh.shape["head"], mesh.shape["stretch"]),
        mesh=mesh,
        in_specs=(placed, placed, placed, P(), P()),
        out_specs=placed,
        check_vma=False,
    )
```

```python
import functools
import math

import jax
import jax.numpy as jnp
from jax import lax
from jax.experimental import pallas as pl
from jax.experimental.pallas import tpu as pltpu
from jax.sharding import PartitionSpec as P

HD = 128
FT = 128
FRAMES = 7
MOT_CAP = 4
NEG = -1e30
MESH = pl.DeviceIdType.MESH

AHEAD = 4
LEAD = 2


def kernel(
    groups, stretches, count, rows, sub,
    frames_ref, motion_ref, q_ref, k_ref, v_ref, out_ref,
    qb, kb, vb, kt, vt, ob, bias,
    in_send, in_recv, in_local, q_send, q_recv, out_send, out_recv, out_local, mot_send, mot_recv,
):
    span = rows * groups
    tail = MOT_CAP * FT
    local = count * HD
    me = lax.axis_index("head")
    stretch = lax.axis_index("stretch")
    has_after = stretch < stretches - 1
    has_before = stretch > 0
    after = jnp.minimum(stretch + 1, stretches - 1)
    before = jnp.maximum(stretch - 1, 0)
    chunks = rows // sub
    live_frames = frames_ref[stretch]
    motion_frames = motion_ref[stretch]

    def peer(offset):
        return lax.rem(me + offset, groups)

    def rows_of(owner):
        return pl.ds(pl.multiple_of(owner * rows, 16), rows)

    def columns(owner, head):
        return pl.ds(pl.multiple_of(owner * local + head * HD, HD), HD)

    def chunk_of(owner, chunk):
        return pl.ds(pl.multiple_of(owner * rows + chunk * sub, 16), sub)

    sources = (k_ref, v_ref, q_ref)
    targets = (kb, vb, qb)

    def exchange(which, head, offset, owner):
        to = peer(offset)
        land = me if owner is None else owner
        return pltpu.make_async_remote_copy(
            src_ref=sources[which].at[:, columns(to, head)],
            dst_ref=targets[which].at[head, rows_of(land), :],
            send_sem=in_send.at[which, head, offset - 1],
            recv_sem=in_recv.at[which, head, offset - 1],
            device_id={"head": to},
            device_id_type=MESH,
        )

    def query(head, offset, chunk, owner):
        to = peer(offset)
        land = me if owner is None else owner
        return pltpu.make_async_remote_copy(
            src_ref=q_ref.at[pl.ds(pl.multiple_of(chunk * sub, 16), sub), columns(to, head)],
            dst_ref=qb.at[head, chunk_of(land, chunk), :],
            send_sem=q_send.at[head, offset - 1, chunk],
            recv_sem=q_recv.at[head, offset - 1, chunk],
            device_id={"head": to},
            device_id_type=MESH,
        )

    def keep(which, head):
        return pltpu.make_async_copy(
            sources[which].at[:, columns(me, head)],
            targets[which].at[head, rows_of(me), :],
            in_local.at[which, head],
        )

    def pass_on(which, head):
        return pltpu.make_async_remote_copy(
            src_ref=(kt, vt)[which].at[head],
            dst_ref=(kb, vb)[which].at[head, pl.ds(span, tail), :],
            send_sem=mot_send.at[which, head],
            recv_sem=mot_recv.at[which, head],
            device_id={"stretch": after},
            device_id_type=MESH,
        )

    def give_back(head, offset, chunk, owner):
        to = peer(offset)
        group = me if owner is None else owner
        return pltpu.make_async_remote_copy(
            src_ref=ob.at[head, chunk_of(to, chunk), :],
            dst_ref=out_ref.at[pl.ds(pl.multiple_of(chunk * sub, 16), sub), columns(group, head)],
            send_sem=out_send.at[head, offset - 1, chunk],
            recv_sem=out_recv.at[head, offset - 1, chunk],
            device_id={"head": to},
            device_id_type=MESH,
        )

    def own_output(head):
        return pltpu.make_async_copy(
            ob.at[head, rows_of(me), :],
            out_ref.at[:, columns(me, head)],
            out_local.at[head],
        )

    def start(which, head):
        for offset in range(1, groups):
            exchange(which, head, offset, None).start()
        keep(which, head).start()

    def arrived(which, head):
        keep(which, head).wait()
        for offset in range(1, groups):
            exchange(which, head, offset, peer(groups - offset)).wait_recv()

    def slot(index):
        @pl.when(index < count)
        def _():
            start(0, index)
            start(1, index)

        @pl.when(jnp.logical_and(index >= LEAD, index < count + LEAD))
        def _():
            for chunk in range(chunks):
                for offset in range(1, groups):
                    query(index - LEAD, offset, chunk, None).start()
            keep(2, index - LEAD).start()

    def forward(head):
        for which, (buffer, ready) in enumerate(((kb, kt), (vb, vt))):
            arrived(which, head)
            for block in range(MOT_CAP):
                chosen = buffer[head, pl.ds(block * FT, FT), :].astype(jnp.float32)
                for skip in range(1, FRAMES - MOT_CAP + 1):
                    other = buffer[head, pl.ds((block + skip) * FT, FT), :].astype(jnp.float32)
                    chosen = jnp.where(live_frames == MOT_CAP + skip, other, chosen)
                ready[head, pl.ds(block * FT, FT), :] = chosen.astype(jnp.bfloat16)

            @pl.when(has_after)
            def _():
                pass_on(which, head).start()

    scale = math.log2(math.e) / math.sqrt(HD)

    def attend(head, base):
        scores = lax.dot_general(
            qb[head, pl.ds(base, sub), :], kb[head],
            (((1,), (1,)), ((), ())), preferred_element_type=jnp.float32,
        )
        scores = scores * scale + bias[...]
        top = jnp.max(scores, axis=1, keepdims=True)
        weights = jnp.exp2(scores - top)
        total = jnp.sum(weights, axis=1, keepdims=True)
        acc = jnp.dot(weights.astype(jnp.bfloat16), vb[head], preferred_element_type=jnp.float32)
        row = base + lax.broadcasted_iota(jnp.int32, (sub, 1), 0)
        mixed = jnp.where(row < live_frames * FT, acc / total, 0.0)
        ob[head, pl.ds(base, sub), :] = mixed.astype(jnp.bfloat16)

    barrier = pltpu.get_barrier_semaphore()
    for offset in range(1, groups):
        pl.semaphore_signal(barrier, inc=1, device_id={"head": peer(offset)}, device_id_type=MESH)
    for other, there in ((after, has_after), (before, has_before)):

        @pl.when(there)
        def _():
            pl.semaphore_signal(barrier, inc=1, device_id={"stretch": other}, device_id_type=MESH)

    pl.semaphore_wait(
        barrier, groups - 1 + has_after.astype(jnp.int32) + has_before.astype(jnp.int32)
    )

    for index in range(AHEAD):
        slot(jnp.int32(index))

    spot = lax.broadcasted_iota(jnp.int32, (1, span + tail), 1)
    own = jnp.logical_and(spot < span, spot < live_frames * FT)
    mot = spot >= span + (MOT_CAP - motion_frames) * FT
    bias[...] = jnp.where(jnp.logical_or(own, mot), 0.0, NEG)

    @pl.when(jnp.logical_not(has_before))
    def _():
        def clear(head, carry):
            for buffer in (kb, vb):
                buffer[head, pl.ds(span, tail), :] = jnp.zeros((tail, HD), jnp.bfloat16)
            return carry

        lax.fori_loop(0, count, clear, 0)

    for head in range(LEAD):
        forward(jnp.int32(head))

    def step(head, carry):
        slot(head + AHEAD)

        @pl.when(head + LEAD < count)
        def _():
            forward(head + LEAD)

        @pl.when(has_before)
        def _():
            for which in range(2):
                pass_on(which, head).wait_recv()

        for offset in range(1, groups):
            to = peer(offset)

            def block(chunk, c):
                query(head, groups - offset, chunk, to).wait_recv()
                attend(head, pl.multiple_of(to * rows + chunk * sub, 16))
                give_back(head, offset, chunk, None).start()
                return c

            lax.fori_loop(0, chunks, block, 0)
        keep(2, head).wait()

        def own_block(chunk, c):
            attend(head, pl.multiple_of(me * rows + chunk * sub, 16))
            return c

        lax.fori_loop(0, chunks, own_block, 0)
        own_output(head).start()
        return carry

    lax.fori_loop(0, count, step, 0)

    def drain(head, carry):
        for offset in range(1, groups):
            for which in range(2):
                exchange(which, head, offset, None).wait_send()
            for chunk in range(chunks):
                query(head, offset, chunk, None).wait_send()
                give_back(head, offset, chunk, None).wait_send()
                give_back(head, offset, chunk, peer(groups - offset)).wait_recv()

        @pl.when(has_after)
        def _():
            for which in range(2):
                pass_on(which, head).wait_send()

        own_output(head).wait()
        return carry

    lax.fori_loop(0, count, drain, 0)


def body(groups, stretches, queries, keys, values, frames, motion):
    rows, width = queries.shape
    span = rows * groups
    tail = MOT_CAP * FT
    local = width // groups
    count = local // HD
    sub = rows // 4 if rows > 256 else rows
    chunks = rows // sub
    wide = jnp.bfloat16
    dma = pltpu.SemaphoreType.DMA
    return pl.pallas_call(
        functools.partial(kernel, groups, stretches, count, rows, sub),
        out_shape=pltpu.VMEM((rows, width), wide),
        in_specs=[pl.BlockSpec(memory_space=pltpu.SMEM)] * 2
        + [pl.BlockSpec(memory_space=pltpu.HBM)] * 3,
        out_specs=pl.BlockSpec(memory_space=pltpu.VMEM),
        scratch_shapes=[
            pltpu.VMEM((count, span, HD), wide),
            pltpu.VMEM((count, span + tail, HD), wide),
            pltpu.VMEM((count, span + tail, HD), wide),
            pltpu.VMEM((count, tail, HD), wide),
            pltpu.VMEM((count, tail, HD), wide),
            pltpu.VMEM((count, span, HD), wide),
            pltpu.VMEM((1, span + tail), jnp.float32),
            dma((2, count, groups - 1)),
            dma((2, count, groups - 1)),
            dma((3, count)),
            dma((count, groups - 1, chunks)),
            dma((count, groups - 1, chunks)),
            dma((count, groups - 1, chunks)),
            dma((count, groups - 1, chunks)),
            dma((count,)),
            dma((2, count)),
            dma((2, count)),
        ],
        compiler_params=pltpu.CompilerParams(
            collective_id=0, has_side_effects=True, vmem_limit_bytes=48 * 1024 * 1024
        ),
        cost_estimate=pl.CostEstimate(
            flops=4 * span * (span + tail) * local,
            bytes_accessed=8 * rows * width,
            transcendentals=span * (span + tail) * count,
        ),
    )(frames, motion, queries, keys, values)


def solution(mesh):
    placed = P(("cfg", "stretch", "head"), None)
    return jax.shard_map(
        functools.partial(body, mesh.shape["head"], mesh.shape["stretch"]),
        mesh=mesh,
        in_specs=(placed, placed, placed, P(), P()),
        out_specs=placed,
        check_vma=False,
    )
```

```python
import functools
import math

import jax
import jax.numpy as jnp
from jax import lax
from jax.experimental import pallas as pl
from jax.experimental.pallas import tpu as pltpu
from jax.sharding import PartitionSpec as P

HD = 128
FT = 128
FRAMES = 7
MOT_CAP = 4
NEG = -1e30
MESH = pl.DeviceIdType.MESH

AHEAD = 4
LAG = 3
LEAD = 2


def kernel(
    groups, stretches, count, rows, sub,
    frames_ref, motion_ref, q_ref, k_ref, v_ref, out_ref,
    qb, kb, vb, kt, vt, ob, bias,
    in_send, in_recv, in_local, q_send, q_recv, out_send, out_recv, out_local, mot_send, mot_recv,
):
    span = rows * groups
    tail = MOT_CAP * FT
    local = count * HD
    me = lax.axis_index("head")
    stretch = lax.axis_index("stretch")
    has_after = stretch < stretches - 1
    has_before = stretch > 0
    after = jnp.minimum(stretch + 1, stretches - 1)
    before = jnp.maximum(stretch - 1, 0)
    chunks = rows // sub
    live_frames = frames_ref[stretch]
    motion_frames = motion_ref[stretch]

    def peer(offset):
        return lax.rem(me + offset, groups)

    def rows_of(owner):
        return pl.ds(pl.multiple_of(owner * rows, 16), rows)

    def columns(owner, head):
        return pl.ds(pl.multiple_of(owner * local + head * HD, HD), HD)

    def chunk_of(owner, chunk):
        return pl.ds(pl.multiple_of(owner * rows + chunk * sub, 16), sub)

    sources = (k_ref, v_ref, q_ref)
    targets = (kb, vb, qb)

    def exchange(which, head, offset, owner):
        to = peer(offset)
        land = me if owner is None else owner
        return pltpu.make_async_remote_copy(
            src_ref=sources[which].at[:, columns(to, head)],
            dst_ref=targets[which].at[head, rows_of(land), :],
            send_sem=in_send.at[which, head, offset - 1],
            recv_sem=in_recv.at[which, head, offset - 1],
            device_id={"head": to},
            device_id_type=MESH,
        )

    def query(head, offset, chunk, owner):
        to = peer(offset)
        land = me if owner is None else owner
        return pltpu.make_async_remote_copy(
            src_ref=q_ref.at[pl.ds(pl.multiple_of(chunk * sub, 16), sub), columns(to, head)],
            dst_ref=qb.at[head, chunk_of(land, chunk), :],
            send_sem=q_send.at[head, offset - 1, chunk],
            recv_sem=q_recv.at[head, offset - 1, chunk],
            device_id={"head": to},
            device_id_type=MESH,
        )

    def keep(which, head):
        return pltpu.make_async_copy(
            sources[which].at[:, columns(me, head)],
            targets[which].at[head, rows_of(me), :],
            in_local.at[which, head],
        )

    def pass_on(which, head):
        return pltpu.make_async_remote_copy(
            src_ref=(kt, vt)[which].at[head],
            dst_ref=(kb, vb)[which].at[head, pl.ds(span, tail), :],
            send_sem=mot_send.at[which, head],
            recv_sem=mot_recv.at[which, head],
            device_id={"stretch": after},
            device_id_type=MESH,
        )

    def give_back(head, offset, chunk, owner):
        to = peer(offset)
        group = me if owner is None else owner
        return pltpu.make_async_remote_copy(
            src_ref=ob.at[head, chunk_of(to, chunk), :],
            dst_ref=out_ref.at[pl.ds(pl.multiple_of(chunk * sub, 16), sub), columns(group, head)],
            send_sem=out_send.at[head, offset - 1, chunk],
            recv_sem=out_recv.at[head, offset - 1, chunk],
            device_id={"head": to},
            device_id_type=MESH,
        )

    def own_output(head):
        return pltpu.make_async_copy(
            ob.at[head, rows_of(me), :],
            out_ref.at[:, columns(me, head)],
            out_local.at[head],
        )

    def start(which, head):
        for offset in range(1, groups):
            exchange(which, head, offset, None).start()
        keep(which, head).start()

    def arrived(which, head):
        keep(which, head).wait()
        for offset in range(1, groups):
            exchange(which, head, offset, peer(groups - offset)).wait_recv()

    def slot(index):
        @pl.when(index < count)
        def _():
            start(0, index)
            start(1, index)

        @pl.when(jnp.logical_and(index >= LEAD, index < count + LEAD))
        def _():
            for chunk in range(chunks):
                for offset in range(1, groups):
                    query(index - LEAD, offset, chunk, None).start()
            keep(2, index - LEAD).start()

    def forward(head):
        for which, (buffer, ready) in enumerate(((kb, kt), (vb, vt))):
            arrived(which, head)
            for block in range(MOT_CAP):
                chosen = buffer[head, pl.ds(block * FT, FT), :].astype(jnp.float32)
                for skip in range(1, FRAMES - MOT_CAP + 1):
                    other = buffer[head, pl.ds((block + skip) * FT, FT), :].astype(jnp.float32)
                    chosen = jnp.where(live_frames == MOT_CAP + skip, other, chosen)
                ready[head, pl.ds(block * FT, FT), :] = chosen.astype(jnp.bfloat16)

            @pl.when(has_after)
            def _():
                pass_on(which, head).start()

    scale = math.log2(math.e) / math.sqrt(HD)

    def attend(head, base):
        scores = lax.dot_general(
            qb[head, pl.ds(base, sub), :], kb[head],
            (((1,), (1,)), ((), ())), preferred_element_type=jnp.float32,
        )
        scores = scores * scale + bias[...]
        top = jnp.max(scores, axis=1, keepdims=True)
        weights = jnp.exp2(scores - top)
        total = jnp.sum(weights, axis=1, keepdims=True)
        acc = jnp.dot(weights.astype(jnp.bfloat16), vb[head], preferred_element_type=jnp.float32)
        row = base + lax.broadcasted_iota(jnp.int32, (sub, 1), 0)
        mixed = jnp.where(row < live_frames * FT, acc / total, 0.0)
        ob[head, pl.ds(base, sub), :] = mixed.astype(jnp.bfloat16)

    barrier = pltpu.get_barrier_semaphore()
    for offset in range(1, groups):
        pl.semaphore_signal(barrier, inc=1, device_id={"head": peer(offset)}, device_id_type=MESH)
    for other, there in ((after, has_after), (before, has_before)):

        @pl.when(there)
        def _():
            pl.semaphore_signal(barrier, inc=1, device_id={"stretch": other}, device_id_type=MESH)

    pl.semaphore_wait(
        barrier, groups - 1 + has_after.astype(jnp.int32) + has_before.astype(jnp.int32)
    )

    for index in range(AHEAD):
        slot(jnp.int32(index))

    spot = lax.broadcasted_iota(jnp.int32, (1, span + tail), 1)
    own = jnp.logical_and(spot < span, spot < live_frames * FT)
    mot = spot >= span + (MOT_CAP - motion_frames) * FT
    bias[...] = jnp.where(jnp.logical_or(own, mot), 0.0, NEG)

    @pl.when(jnp.logical_not(has_before))
    def _():
        def clear(head, carry):
            for buffer in (kb, vb):
                buffer[head, pl.ds(span, tail), :] = jnp.zeros((tail, HD), jnp.bfloat16)
            return carry

        lax.fori_loop(0, count, clear, 0)

    for head in range(LEAD):
        forward(jnp.int32(head))

    def drain(head):
        for offset in range(1, groups):
            for which in range(2):
                exchange(which, head, offset, None).wait_send()
            for chunk in range(chunks):
                query(head, offset, chunk, None).wait_send()
                give_back(head, offset, chunk, None).wait_send()
                give_back(head, offset, chunk, peer(groups - offset)).wait_recv()

        @pl.when(has_after)
        def _():
            for which in range(2):
                pass_on(which, head).wait_send()

        own_output(head).wait()

    def step(head, carry):
        slot(head + AHEAD)

        @pl.when(head + LEAD < count)
        def _():
            forward(head + LEAD)

        @pl.when(has_before)
        def _():
            for which in range(2):
                pass_on(which, head).wait_recv()

        for offset in range(1, groups):
            to = peer(offset)

            def block(chunk, c):
                query(head, groups - offset, chunk, to).wait_recv()
                attend(head, pl.multiple_of(to * rows + chunk * sub, 16))
                give_back(head, offset, chunk, None).start()
                return c

            lax.fori_loop(0, chunks, block, 0)
        keep(2, head).wait()

        def own_block(chunk, c):
            attend(head, pl.multiple_of(me * rows + chunk * sub, 16))
            return c

        lax.fori_loop(0, chunks, own_block, 0)
        own_output(head).start()

        @pl.when(head >= LAG)
        def _():
            drain(head - LAG)

        return carry

    lax.fori_loop(0, count, step, 0)

    def last(head, carry):
        drain(head)
        return carry

    lax.fori_loop(max(count - LAG, 0), count, last, 0)


def body(groups, stretches, queries, keys, values, frames, motion):
    rows, width = queries.shape
    span = rows * groups
    tail = MOT_CAP * FT
    local = width // groups
    count = local // HD
    sub = rows // 4 if rows > 256 else rows
    chunks = rows // sub
    wide = jnp.bfloat16
    dma = pltpu.SemaphoreType.DMA
    return pl.pallas_call(
        functools.partial(kernel, groups, stretches, count, rows, sub),
        out_shape=pltpu.VMEM((rows, width), wide),
        in_specs=[pl.BlockSpec(memory_space=pltpu.SMEM)] * 2
        + [pl.BlockSpec(memory_space=pltpu.HBM)] * 3,
        out_specs=pl.BlockSpec(memory_space=pltpu.VMEM),
        scratch_shapes=[
            pltpu.VMEM((count, span, HD), wide),
            pltpu.VMEM((count, span + tail, HD), wide),
            pltpu.VMEM((count, span + tail, HD), wide),
            pltpu.VMEM((count, tail, HD), wide),
            pltpu.VMEM((count, tail, HD), wide),
            pltpu.VMEM((count, span, HD), wide),
            pltpu.VMEM((1, span + tail), jnp.float32),
            dma((2, count, groups - 1)),
            dma((2, count, groups - 1)),
            dma((3, count)),
            dma((count, groups - 1, chunks)),
            dma((count, groups - 1, chunks)),
            dma((count, groups - 1, chunks)),
            dma((count, groups - 1, chunks)),
            dma((count,)),
            dma((2, count)),
            dma((2, count)),
        ],
        compiler_params=pltpu.CompilerParams(
            collective_id=0, has_side_effects=True, vmem_limit_bytes=58 * 1024 * 1024
        ),
        cost_estimate=pl.CostEstimate(
            flops=4 * span * (span + tail) * local,
            bytes_accessed=8 * rows * width,
            transcendentals=span * (span + tail) * count,
        ),
    )(frames, motion, queries, keys, values)


def solution(mesh):
    placed = P(("cfg", "stretch", "head"), None)
    return jax.shard_map(
        functools.partial(body, mesh.shape["head"], mesh.shape["stretch"]),
        mesh=mesh,
        in_specs=(placed, placed, placed, P(), P()),
        out_specs=placed,
        check_vma=False,
    )
```

```python
import functools
import math

import jax
import jax.numpy as jnp
from jax import lax
from jax.experimental import pallas as pl
from jax.experimental.pallas import tpu as pltpu
from jax.sharding import PartitionSpec as P

HD = 128
FT = 128
FRAMES = 7
MOT_CAP = 4
NEG = -1e30
MESH = pl.DeviceIdType.MESH

PACK = 2
AHEAD = 3
LEAD = 1
LAG = 2


def kernel(
    groups, stretches, count, pack, rows, sub,
    frames_ref, motion_ref, q_ref, k_ref, v_ref, out_ref,
    qb, kb, vb, kt, vt, ob, bias,
    in_send, in_recv, in_local, q_send, q_recv, out_send, out_recv, out_local, mot_send, mot_recv,
):
    span = rows * groups
    tail = MOT_CAP * FT
    unit = pack * HD
    local = count * unit
    fine = rows // sub
    me = lax.axis_index("head")
    stretch = lax.axis_index("stretch")
    has_after = stretch < stretches - 1
    has_before = stretch > 0
    after = jnp.minimum(stretch + 1, stretches - 1)
    before = jnp.maximum(stretch - 1, 0)
    live_frames = frames_ref[stretch]
    motion_frames = motion_ref[stretch]

    def peer(offset):
        return lax.rem(me + offset, groups)

    def columns(owner, index):
        return pl.ds(pl.multiple_of(owner * local + index * unit, unit), unit)

    def part_rows(base, part, parts):
        size = rows // parts
        return pl.ds(pl.multiple_of(base + part * size, 16), size)

    sources = (k_ref, v_ref, q_ref)
    targets = (kb, vb, qb)

    def exchange(which, index, offset, owner):
        to = peer(offset)
        land = me if owner is None else owner
        return pltpu.make_async_remote_copy(
            src_ref=sources[which].at[:, columns(to, index)],
            dst_ref=targets[which].at[index, part_rows(land * rows, 0, 1), :],
            send_sem=in_send.at[which, index, offset - 1],
            recv_sem=in_recv.at[which, index, offset - 1],
            device_id={"head": to},
            device_id_type=MESH,
        )

    def query(index, offset, owner, part, parts):
        to = peer(offset)
        land = me if owner is None else owner
        return pltpu.make_async_remote_copy(
            src_ref=q_ref.at[part_rows(0, part, parts), columns(to, index)],
            dst_ref=qb.at[index, part_rows(land * rows, part, parts), :],
            send_sem=q_send.at[index, offset - 1, part],
            recv_sem=q_recv.at[index, offset - 1, part],
            device_id={"head": to},
            device_id_type=MESH,
        )

    def keep(which, index):
        return pltpu.make_async_copy(
            sources[which].at[:, columns(me, index)],
            targets[which].at[index, part_rows(me * rows, 0, 1), :],
            in_local.at[which, index],
        )

    def pass_on(which, index):
        return pltpu.make_async_remote_copy(
            src_ref=(kt, vt)[which].at[index],
            dst_ref=(kb, vb)[which].at[index, pl.ds(span, tail), :],
            send_sem=mot_send.at[which, index],
            recv_sem=mot_recv.at[which, index],
            device_id={"stretch": after},
            device_id_type=MESH,
        )

    def give_back(index, offset, owner, part, parts):
        to = peer(offset)
        group = me if owner is None else owner
        return pltpu.make_async_remote_copy(
            src_ref=ob.at[index, part_rows(to * rows, part, parts), :],
            dst_ref=out_ref.at[part_rows(0, part, parts), columns(group, index)],
            send_sem=out_send.at[index, offset - 1, part],
            recv_sem=out_recv.at[index, offset - 1, part],
            device_id={"head": to},
            device_id_type=MESH,
        )

    def own_output(index):
        return pltpu.make_async_copy(
            ob.at[index, part_rows(me * rows, 0, 1), :],
            out_ref.at[:, columns(me, index)],
            out_local.at[index],
        )

    def send_queries(index, parts):
        for part in range(parts):
            for offset in range(1, groups):
                query(index, offset, None, part, parts).start()
        keep(2, index).start()

    def slot(index):
        @pl.when(index < count)
        def _():
            for which in range(2):
                for offset in range(1, groups):
                    exchange(which, index, offset, None).start()
                keep(which, index).start()

        @pl.when(jnp.logical_and(index >= LEAD, index < count + LEAD - 1))
        def _():
            send_queries(index - LEAD, 1)

        @pl.when(index == count + LEAD - 1)
        def _():
            send_queries(count - 1, fine)

    def forward(index):
        for which, (buffer, ready) in enumerate(((kb, kt), (vb, vt))):
            keep(which, index).wait()
            for offset in range(1, groups):
                exchange(which, index, offset, peer(groups - offset)).wait_recv()
            for block in range(MOT_CAP):
                chosen = buffer[index, pl.ds(block * FT, FT), :].astype(jnp.float32)
                for skip in range(1, FRAMES - MOT_CAP + 1):
                    other = buffer[index, pl.ds((block + skip) * FT, FT), :].astype(jnp.float32)
                    chosen = jnp.where(live_frames == MOT_CAP + skip, other, chosen)
                ready[index, pl.ds(block * FT, FT), :] = chosen.astype(jnp.bfloat16)

            @pl.when(has_after)
            def _():
                pass_on(which, index).start()

    scale = math.log2(math.e) / math.sqrt(HD)

    def attend(index, base):
        row = base + lax.broadcasted_iota(jnp.int32, (sub, 1), 0)
        for head in range(pack):
            lanes = slice(head * HD, (head + 1) * HD)
            scores = lax.dot_general(
                qb[index, pl.ds(base, sub), lanes], kb[index, :, lanes],
                (((1,), (1,)), ((), ())), preferred_element_type=jnp.float32,
            )
            scores = scores * scale + bias[...]
            top = jnp.max(scores, axis=1, keepdims=True)
            weights = jnp.exp2(scores - top)
            total = jnp.sum(weights, axis=1, keepdims=True)
            acc = jnp.dot(
                weights.astype(jnp.bfloat16), vb[index, :, lanes],
                preferred_element_type=jnp.float32,
            )
            mixed = jnp.where(row < live_frames * FT, acc / total, 0.0)
            ob[index, pl.ds(base, sub), lanes] = mixed.astype(jnp.bfloat16)

    def attend_rows(index, begin, number):
        def block(step, carry):
            attend(index, pl.multiple_of(begin + step * sub, 16))
            return carry

        lax.fori_loop(0, number, block, 0)

    barrier = pltpu.get_barrier_semaphore()
    for offset in range(1, groups):
        pl.semaphore_signal(barrier, inc=1, device_id={"head": peer(offset)}, device_id_type=MESH)
    for other, there in ((after, has_after), (before, has_before)):

        @pl.when(there)
        def _():
            pl.semaphore_signal(barrier, inc=1, device_id={"stretch": other}, device_id_type=MESH)

    pl.semaphore_wait(
        barrier, groups - 1 + has_after.astype(jnp.int32) + has_before.astype(jnp.int32)
    )

    for index in range(AHEAD):
        slot(jnp.int32(index))

    spot = lax.broadcasted_iota(jnp.int32, (1, span + tail), 1)
    own = jnp.logical_and(spot < span, spot < live_frames * FT)
    mot = spot >= span + (MOT_CAP - motion_frames) * FT
    bias[...] = jnp.where(jnp.logical_or(own, mot), 0.0, NEG)

    @pl.when(jnp.logical_not(has_before))
    def _():
        def clear(index, carry):
            for buffer in (kb, vb):
                buffer[index, pl.ds(span, tail), :] = jnp.zeros((tail, unit), jnp.bfloat16)
            return carry

        lax.fori_loop(0, count, clear, 0)

    for index in range(LEAD):
        forward(jnp.int32(index))

    def work(index, parts):
        slot(index + AHEAD)

        @pl.when(index + LEAD < count)
        def _():
            forward(index + LEAD)

        @pl.when(has_before)
        def _():
            for which in range(2):
                pass_on(which, index).wait_recv()

        keep(2, index).wait()
        attend_rows(index, me * rows, fine)
        own_output(index).start()
        for offset in range(1, groups):
            to = peer(offset)

            def chunk(part, carry):
                query(index, groups - offset, to, part, parts).wait_recv()
                attend_rows(index, to * rows + part * (rows // parts), fine // parts)
                give_back(index, offset, None, part, parts).start()
                return carry

            lax.fori_loop(0, parts, chunk, 0)

    def retire(index, parts):
        for offset in range(1, groups):
            for which in range(2):
                exchange(which, index, offset, None).wait_send()
            for part in range(parts):
                query(index, offset, None, part, parts).wait_send()
                give_back(index, offset, None, part, parts).wait_send()
                give_back(index, offset, peer(groups - offset), part, parts).wait_recv()

        @pl.when(has_after)
        def _():
            for which in range(2):
                pass_on(which, index).wait_send()

        own_output(index).wait()

    def step(index, carry):
        work(index, 1)

        @pl.when(index >= LAG)
        def _():
            retire(index - LAG, 1)

        return carry

    lax.fori_loop(0, count - 1, step, 0)
    work(jnp.int32(count - 1), fine)
    for index in range(max(count - 1 - LAG, 0), count - 1):
        retire(jnp.int32(index), 1)
    retire(jnp.int32(count - 1), fine)


def body(groups, stretches, queries, keys, values, frames, motion):
    rows, width = queries.shape
    span = rows * groups
    tail = MOT_CAP * FT
    local = width // groups
    heads = local // HD
    pack = math.gcd(heads, PACK)
    count = heads // pack
    unit = pack * HD
    sub = rows // 4 if rows % 64 == 0 else rows
    fine = rows // sub
    wide = jnp.bfloat16
    dma = pltpu.SemaphoreType.DMA
    return pl.pallas_call(
        functools.partial(kernel, groups, stretches, count, pack, rows, sub),
        out_shape=pltpu.VMEM((rows, width), wide),
        in_specs=[pl.BlockSpec(memory_space=pltpu.SMEM)] * 2
        + [pl.BlockSpec(memory_space=pltpu.HBM)] * 3,
        out_specs=pl.BlockSpec(memory_space=pltpu.VMEM),
        scratch_shapes=[
            pltpu.VMEM((count, span, unit), wide),
            pltpu.VMEM((count, span + tail, unit), wide),
            pltpu.VMEM((count, span + tail, unit), wide),
            pltpu.VMEM((count, tail, unit), wide),
            pltpu.VMEM((count, tail, unit), wide),
            pltpu.VMEM((count, span, unit), wide),
            pltpu.VMEM((1, span + tail), jnp.float32),
            dma((2, count, groups - 1)),
            dma((2, count, groups - 1)),
            dma((3, count)),
            dma((count, groups - 1, fine)),
            dma((count, groups - 1, fine)),
            dma((count, groups - 1, fine)),
            dma((count, groups - 1, fine)),
            dma((count,)),
            dma((2, count)),
            dma((2, count)),
        ],
        compiler_params=pltpu.CompilerParams(
            collective_id=0, has_side_effects=True, vmem_limit_bytes=58 * 1024 * 1024
        ),
        cost_estimate=pl.CostEstimate(
            flops=4 * span * (span + tail) * local,
            bytes_accessed=8 * rows * width,
            transcendentals=span * (span + tail) * heads,
        ),
    )(frames, motion, queries, keys, values)


def solution(mesh):
    placed = P(("cfg", "stretch", "head"), None)
    return jax.shard_map(
        functools.partial(body, mesh.shape["head"], mesh.shape["stretch"]),
        mesh=mesh,
        in_specs=(placed, placed, placed, P(), P()),
        out_specs=placed,
        check_vma=False,
    )
```

```python
import functools
import math

import jax
import jax.numpy as jnp
from jax import lax
from jax.experimental import pallas as pl
from jax.experimental.pallas import tpu as pltpu
from jax.sharding import PartitionSpec as P

HD = 128
FT = 128
FRAMES = 7
MOT_CAP = 4
NEG = -1e30
MESH = pl.DeviceIdType.MESH

PACK = 2
AHEAD = 4
LEAD = 2
LAG = 2


def kernel(
    groups, stretches, count, pack, rows, sub,
    frames_ref, motion_ref, q_ref, k_ref, v_ref, out_ref,
    qb, kb, vb, kt, vt, ob, bias,
    in_send, in_recv, in_local, q_send, q_recv, out_send, out_recv, out_local, mot_send, mot_recv,
):
    span = rows * groups
    tail = MOT_CAP * FT
    unit = pack * HD
    local = count * unit
    fine = rows // sub
    me = lax.axis_index("head")
    stretch = lax.axis_index("stretch")
    has_after = stretch < stretches - 1
    has_before = stretch > 0
    after = jnp.minimum(stretch + 1, stretches - 1)
    before = jnp.maximum(stretch - 1, 0)
    live_frames = frames_ref[stretch]
    motion_frames = motion_ref[stretch]

    def peer(offset):
        return lax.rem(me + offset, groups)

    def columns(owner, index):
        return pl.ds(pl.multiple_of(owner * local + index * unit, unit), unit)

    def part_rows(base, part, parts):
        size = rows // parts
        return pl.ds(pl.multiple_of(base + part * size, 16), size)

    sources = (k_ref, v_ref, q_ref)
    targets = (kb, vb, qb)

    def exchange(which, index, offset, owner):
        to = peer(offset)
        land = me if owner is None else owner
        return pltpu.make_async_remote_copy(
            src_ref=sources[which].at[:, columns(to, index)],
            dst_ref=targets[which].at[index, part_rows(land * rows, 0, 1), :],
            send_sem=in_send.at[which, index, offset - 1],
            recv_sem=in_recv.at[which, index, offset - 1],
            device_id={"head": to},
            device_id_type=MESH,
        )

    def query(index, offset, owner, part, parts):
        to = peer(offset)
        land = me if owner is None else owner
        return pltpu.make_async_remote_copy(
            src_ref=q_ref.at[part_rows(0, part, parts), columns(to, index)],
            dst_ref=qb.at[index, part_rows(land * rows, part, parts), :],
            send_sem=q_send.at[index, offset - 1, part],
            recv_sem=q_recv.at[index, offset - 1, part],
            device_id={"head": to},
            device_id_type=MESH,
        )

    def keep(which, index):
        return pltpu.make_async_copy(
            sources[which].at[:, columns(me, index)],
            targets[which].at[index, part_rows(me * rows, 0, 1), :],
            in_local.at[which, index],
        )

    def pass_on(which, index):
        return pltpu.make_async_remote_copy(
            src_ref=(kt, vt)[which].at[index],
            dst_ref=(kb, vb)[which].at[index, pl.ds(span, tail), :],
            send_sem=mot_send.at[which, index],
            recv_sem=mot_recv.at[which, index],
            device_id={"stretch": after},
            device_id_type=MESH,
        )

    def give_back(index, offset, owner, part, parts):
        to = peer(offset)
        group = me if owner is None else owner
        return pltpu.make_async_remote_copy(
            src_ref=ob.at[index, part_rows(to * rows, part, parts), :],
            dst_ref=out_ref.at[part_rows(0, part, parts), columns(group, index)],
            send_sem=out_send.at[index, offset - 1, part],
            recv_sem=out_recv.at[index, offset - 1, part],
            device_id={"head": to},
            device_id_type=MESH,
        )

    def own_output(index):
        return pltpu.make_async_copy(
            ob.at[index, part_rows(me * rows, 0, 1), :],
            out_ref.at[:, columns(me, index)],
            out_local.at[index],
        )

    def send_queries(index, parts):
        for part in range(parts):
            for offset in range(1, groups):
                query(index, offset, None, part, parts).start()
        keep(2, index).start()

    def slot(index):
        @pl.when(index < count)
        def _():
            for which in range(2):
                for offset in range(1, groups):
                    exchange(which, index, offset, None).start()
                keep(which, index).start()

        @pl.when(jnp.logical_and(index >= LEAD, index < count + LEAD - 1))
        def _():
            send_queries(index - LEAD, 1)

        @pl.when(index == count + LEAD - 1)
        def _():
            send_queries(count - 1, fine)

    def forward(index):
        for which, (buffer, ready) in enumerate(((kb, kt), (vb, vt))):
            keep(which, index).wait()
            for offset in range(1, groups):
                exchange(which, index, offset, peer(groups - offset)).wait_recv()
            for block in range(MOT_CAP):
                chosen = buffer[index, pl.ds(block * FT, FT), :].astype(jnp.float32)
                for skip in range(1, FRAMES - MOT_CAP + 1):
                    other = buffer[index, pl.ds((block + skip) * FT, FT), :].astype(jnp.float32)
                    chosen = jnp.where(live_frames == MOT_CAP + skip, other, chosen)
                ready[index, pl.ds(block * FT, FT), :] = chosen.astype(jnp.bfloat16)

            @pl.when(has_after)
            def _():
                pass_on(which, index).start()

    scale = math.log2(math.e) / math.sqrt(HD)

    def attend(index, base):
        row = base + lax.broadcasted_iota(jnp.int32, (sub, 1), 0)
        for head in range(pack):
            lanes = slice(head * HD, (head + 1) * HD)
            scores = lax.dot_general(
                qb[index, pl.ds(base, sub), lanes], kb[index, :, lanes],
                (((1,), (1,)), ((), ())), preferred_element_type=jnp.float32,
            )
            scores = scores * scale + bias[...]
            top = jnp.max(scores, axis=1, keepdims=True)
            weights = jnp.exp2(scores - top)
            total = jnp.sum(weights, axis=1, keepdims=True)
            acc = jnp.dot(
                weights.astype(jnp.bfloat16), vb[index, :, lanes],
                preferred_element_type=jnp.float32,
            )
            mixed = jnp.where(row < live_frames * FT, acc / total, 0.0)
            ob[index, pl.ds(base, sub), lanes] = mixed.astype(jnp.bfloat16)

    def attend_rows(index, begin, number):
        def block(step, carry):
            attend(index, pl.multiple_of(begin + step * sub, 16))
            return carry

        lax.fori_loop(0, number, block, 0)

    barrier = pltpu.get_barrier_semaphore()
    for offset in range(1, groups):
        pl.semaphore_signal(barrier, inc=1, device_id={"head": peer(offset)}, device_id_type=MESH)
    for other, there in ((after, has_after), (before, has_before)):

        @pl.when(there)
        def _():
            pl.semaphore_signal(barrier, inc=1, device_id={"stretch": other}, device_id_type=MESH)

    pl.semaphore_wait(
        barrier, groups - 1 + has_after.astype(jnp.int32) + has_before.astype(jnp.int32)
    )

    for index in range(AHEAD):
        slot(jnp.int32(index))

    spot = lax.broadcasted_iota(jnp.int32, (1, span + tail), 1)
    own = jnp.logical_and(spot < span, spot < live_frames * FT)
    mot = spot >= span + (MOT_CAP - motion_frames) * FT
    bias[...] = jnp.where(jnp.logical_or(own, mot), 0.0, NEG)

    @pl.when(jnp.logical_not(has_before))
    def _():
        def clear(index, carry):
            for buffer in (kb, vb):
                buffer[index, pl.ds(span, tail), :] = jnp.zeros((tail, unit), jnp.bfloat16)
            return carry

        lax.fori_loop(0, count, clear, 0)

    for index in range(LEAD):
        forward(jnp.int32(index))

    def work(index, parts):
        slot(index + AHEAD)

        @pl.when(index + LEAD < count)
        def _():
            forward(index + LEAD)

        @pl.when(has_before)
        def _():
            for which in range(2):
                pass_on(which, index).wait_recv()

        keep(2, index).wait()
        attend_rows(index, me * rows, fine)
        own_output(index).start()
        for offset in range(1, groups):
            to = peer(offset)

            def chunk(part, carry):
                query(index, groups - offset, to, part, parts).wait_recv()
                attend_rows(index, to * rows + part * (rows // parts), fine // parts)
                give_back(index, offset, None, part, parts).start()
                return carry

            lax.fori_loop(0, parts, chunk, 0)

    def retire(index, parts):
        for offset in range(1, groups):
            for which in range(2):
                exchange(which, index, offset, None).wait_send()
            for part in range(parts):
                query(index, offset, None, part, parts).wait_send()
                give_back(index, offset, None, part, parts).wait_send()
                give_back(index, offset, peer(groups - offset), part, parts).wait_recv()

        @pl.when(has_after)
        def _():
            for which in range(2):
                pass_on(which, index).wait_send()

        own_output(index).wait()

    def step(index, carry):
        work(index, 1)

        @pl.when(index >= LAG)
        def _():
            retire(index - LAG, 1)

        return carry

    lax.fori_loop(0, count - 1, step, 0)
    work(jnp.int32(count - 1), fine)
    for index in range(max(count - 1 - LAG, 0), count - 1):
        retire(jnp.int32(index), 1)
    retire(jnp.int32(count - 1), fine)


def body(groups, stretches, queries, keys, values, frames, motion):
    rows, width = queries.shape
    span = rows * groups
    tail = MOT_CAP * FT
    local = width // groups
    heads = local // HD
    pack = math.gcd(heads, PACK)
    count = heads // pack
    unit = pack * HD
    sub = rows // 4 if rows % 64 == 0 else rows
    fine = rows // sub
    wide = jnp.bfloat16
    dma = pltpu.SemaphoreType.DMA
    return pl.pallas_call(
        functools.partial(kernel, groups, stretches, count, pack, rows, sub),
        out_shape=pltpu.VMEM((rows, width), wide),
        in_specs=[pl.BlockSpec(memory_space=pltpu.SMEM)] * 2
        + [pl.BlockSpec(memory_space=pltpu.HBM)] * 3,
        out_specs=pl.BlockSpec(memory_space=pltpu.VMEM),
        scratch_shapes=[
            pltpu.VMEM((count, span, unit), wide),
            pltpu.VMEM((count, span + tail, unit), wide),
            pltpu.VMEM((count, span + tail, unit), wide),
            pltpu.VMEM((count, tail, unit), wide),
            pltpu.VMEM((count, tail, unit), wide),
            pltpu.VMEM((count, span, unit), wide),
            pltpu.VMEM((1, span + tail), jnp.float32),
            dma((2, count, groups - 1)),
            dma((2, count, groups - 1)),
            dma((3, count)),
            dma((count, groups - 1, fine)),
            dma((count, groups - 1, fine)),
            dma((count, groups - 1, fine)),
            dma((count, groups - 1, fine)),
            dma((count,)),
            dma((2, count)),
            dma((2, count)),
        ],
        compiler_params=pltpu.CompilerParams(
            collective_id=0, has_side_effects=True, vmem_limit_bytes=58 * 1024 * 1024
        ),
        cost_estimate=pl.CostEstimate(
            flops=4 * span * (span + tail) * local,
            bytes_accessed=8 * rows * width,
            transcendentals=span * (span + tail) * heads,
        ),
    )(frames, motion, queries, keys, values)


def solution(mesh):
    placed = P(("cfg", "stretch", "head"), None)
    return jax.shard_map(
        functools.partial(body, mesh.shape["head"], mesh.shape["stretch"]),
        mesh=mesh,
        in_specs=(placed, placed, placed, P(), P()),
        out_specs=placed,
        check_vma=False,
    )
```

```python
import functools
import math

import jax
import jax.numpy as jnp
from jax import lax
from jax.experimental import pallas as pl
from jax.experimental.pallas import tpu as pltpu
from jax.sharding import PartitionSpec as P

HD = 128
FT = 128
FRAMES = 7
MOT_CAP = 4
NEG = -1e30
MESH = pl.DeviceIdType.MESH

PACK = 4
AHEAD = 2
LEAD = 1
LAG = 1


def kernel(
    groups, stretches, count, pack, rows, fine, sub,
    frames_ref, motion_ref, q_ref, k_ref, v_ref, out_ref,
    qb, kb, vb, kt, vt, ob, bias,
    in_send, in_recv, in_local, q_send, q_recv, out_send, out_recv, out_local, mot_send, mot_recv,
):
    span = rows * groups
    tail = MOT_CAP * FT
    unit = pack * HD
    local = count * unit
    me = lax.axis_index("head")
    stretch = lax.axis_index("stretch")
    has_after = stretch < stretches - 1
    has_before = stretch > 0
    after = jnp.minimum(stretch + 1, stretches - 1)
    before = jnp.maximum(stretch - 1, 0)
    live_frames = frames_ref[stretch]
    motion_frames = motion_ref[stretch]

    def peer(offset):
        return lax.rem(me + offset, groups)

    def columns(owner, index):
        return pl.ds(pl.multiple_of(owner * local + index * unit, unit), unit)

    def part_rows(base, part, parts):
        size = rows // parts
        return pl.ds(pl.multiple_of(base + part * size, 16), size)

    sources = (k_ref, v_ref, q_ref)
    targets = (kb, vb, qb)

    def exchange(which, index, offset, owner):
        to = peer(offset)
        land = me if owner is None else owner
        return pltpu.make_async_remote_copy(
            src_ref=sources[which].at[:, columns(to, index)],
            dst_ref=targets[which].at[index, part_rows(land * rows, 0, 1), :],
            send_sem=in_send.at[which, index, offset - 1],
            recv_sem=in_recv.at[which, index, offset - 1],
            device_id={"head": to},
            device_id_type=MESH,
        )

    def query(index, offset, owner, part, parts):
        to = peer(offset)
        land = me if owner is None else owner
        return pltpu.make_async_remote_copy(
            src_ref=q_ref.at[part_rows(0, part, parts), columns(to, index)],
            dst_ref=qb.at[index, part_rows(land * rows, part, parts), :],
            send_sem=q_send.at[index, offset - 1, part],
            recv_sem=q_recv.at[index, offset - 1, part],
            device_id={"head": to},
            device_id_type=MESH,
        )

    def keep(which, index):
        return pltpu.make_async_copy(
            sources[which].at[:, columns(me, index)],
            targets[which].at[index, part_rows(me * rows, 0, 1), :],
            in_local.at[which, index],
        )

    def pass_on(which, index):
        return pltpu.make_async_remote_copy(
            src_ref=(kt, vt)[which].at[index],
            dst_ref=(kb, vb)[which].at[index, pl.ds(span, tail), :],
            send_sem=mot_send.at[which, index],
            recv_sem=mot_recv.at[which, index],
            device_id={"stretch": after},
            device_id_type=MESH,
        )

    def give_back(index, offset, owner, part, parts):
        to = peer(offset)
        group = me if owner is None else owner
        return pltpu.make_async_remote_copy(
            src_ref=ob.at[index, part_rows(to * rows, part, parts), :],
            dst_ref=out_ref.at[part_rows(0, part, parts), columns(group, index)],
            send_sem=out_send.at[index, offset - 1, part],
            recv_sem=out_recv.at[index, offset - 1, part],
            device_id={"head": to},
            device_id_type=MESH,
        )

    def own_output(index):
        return pltpu.make_async_copy(
            ob.at[index, part_rows(me * rows, 0, 1), :],
            out_ref.at[:, columns(me, index)],
            out_local.at[index],
        )

    def send_queries(index, parts):
        for part in range(parts):
            for offset in range(1, groups):
                query(index, offset, None, part, parts).start()
        keep(2, index).start()

    def slot(index):
        @pl.when(index < count)
        def _():
            for which in range(2):
                for offset in range(1, groups):
                    exchange(which, index, offset, None).start()
                keep(which, index).start()

        @pl.when(jnp.logical_and(index >= LEAD, index < count + LEAD - 1))
        def _():
            send_queries(index - LEAD, 1)

        @pl.when(index == count + LEAD - 1)
        def _():
            send_queries(count - 1, fine)

    def forward(index):
        for which, (buffer, ready) in enumerate(((kb, kt), (vb, vt))):
            keep(which, index).wait()
            for offset in range(1, groups):
                exchange(which, index, offset, peer(groups - offset)).wait_recv()
            for block in range(MOT_CAP):
                chosen = buffer[index, pl.ds(block * FT, FT), :].astype(jnp.float32)
                for skip in range(1, FRAMES - MOT_CAP + 1):
                    other = buffer[index, pl.ds((block + skip) * FT, FT), :].astype(jnp.float32)
                    chosen = jnp.where(live_frames == MOT_CAP + skip, other, chosen)
                ready[index, pl.ds(block * FT, FT), :] = chosen.astype(jnp.bfloat16)

            @pl.when(has_after)
            def _():
                pass_on(which, index).start()

    scale = math.log2(math.e) / math.sqrt(HD)

    def attend(index, base, size):
        row = base + lax.broadcasted_iota(jnp.int32, (size, 1), 0)
        for head in range(pack):
            lanes = slice(head * HD, (head + 1) * HD)
            scores = lax.dot_general(
                qb[index, pl.ds(base, size), lanes], kb[index, :, lanes],
                (((1,), (1,)), ((), ())), preferred_element_type=jnp.float32,
            )
            scores = scores * scale + bias[...]
            top = jnp.max(scores, axis=1, keepdims=True)
            weights = jnp.exp2(scores - top)
            total = jnp.sum(weights, axis=1, keepdims=True)
            acc = jnp.dot(
                weights.astype(jnp.bfloat16), vb[index, :, lanes],
                preferred_element_type=jnp.float32,
            )
            mixed = jnp.where(row < live_frames * FT, acc / total, 0.0)
            ob[index, pl.ds(base, size), lanes] = mixed.astype(jnp.bfloat16)

    def attend_rows(index, begin, number):
        size = min(sub, number)

        def block(step, carry):
            attend(index, pl.multiple_of(begin + step * size, 16), size)
            return carry

        lax.fori_loop(0, number // size, block, 0)

    barrier = pltpu.get_barrier_semaphore()
    for offset in range(1, groups):
        pl.semaphore_signal(barrier, inc=1, device_id={"head": peer(offset)}, device_id_type=MESH)
    for other, there in ((after, has_after), (before, has_before)):

        @pl.when(there)
        def _():
            pl.semaphore_signal(barrier, inc=1, device_id={"stretch": other}, device_id_type=MESH)

    pl.semaphore_wait(
        barrier, groups - 1 + has_after.astype(jnp.int32) + has_before.astype(jnp.int32)
    )

    for index in range(AHEAD):
        slot(jnp.int32(index))

    spot = lax.broadcasted_iota(jnp.int32, (1, span + tail), 1)
    own = jnp.logical_and(spot < span, spot < live_frames * FT)
    mot = spot >= span + (MOT_CAP - motion_frames) * FT
    bias[...] = jnp.where(jnp.logical_or(own, mot), 0.0, NEG)

    @pl.when(jnp.logical_not(has_before))
    def _():
        def clear(index, carry):
            for buffer in (kb, vb):
                buffer[index, pl.ds(span, tail), :] = jnp.zeros((tail, unit), jnp.bfloat16)
            return carry

        lax.fori_loop(0, count, clear, 0)

    for index in range(LEAD):
        forward(jnp.int32(index))

    def work(index, parts):
        slot(index + AHEAD)

        @pl.when(index + LEAD < count)
        def _():
            forward(index + LEAD)

        @pl.when(has_before)
        def _():
            for which in range(2):
                pass_on(which, index).wait_recv()

        keep(2, index).wait()
        attend_rows(index, me * rows, rows)
        own_output(index).start()
        for offset in range(1, groups):
            to = peer(offset)

            def chunk(part, carry):
                query(index, groups - offset, to, part, parts).wait_recv()
                attend_rows(index, to * rows + part * (rows // parts), rows // parts)
                give_back(index, offset, None, part, parts).start()
                return carry

            lax.fori_loop(0, parts, chunk, 0)

    def retire(index, parts):
        for offset in range(1, groups):
            for which in range(2):
                exchange(which, index, offset, None).wait_send()
            for part in range(parts):
                query(index, offset, None, part, parts).wait_send()
                give_back(index, offset, None, part, parts).wait_send()
                give_back(index, offset, peer(groups - offset), part, parts).wait_recv()

        @pl.when(has_after)
        def _():
            for which in range(2):
                pass_on(which, index).wait_send()

        own_output(index).wait()

    def step(index, carry):
        work(index, 1)

        @pl.when(index >= LAG)
        def _():
            retire(index - LAG, 1)

        return carry

    lax.fori_loop(0, count - 1, step, 0)
    work(jnp.int32(count - 1), fine)
    for index in range(max(count - 1 - LAG, 0), count - 1):
        retire(jnp.int32(index), 1)
    retire(jnp.int32(count - 1), fine)


def body(groups, stretches, queries, keys, values, frames, motion):
    rows, width = queries.shape
    span = rows * groups
    tail = MOT_CAP * FT
    local = width // groups
    heads = local // HD
    pack = math.gcd(heads, PACK)
    count = heads // pack
    unit = pack * HD
    sub = rows // 4 if rows % 64 == 0 else rows
    fine = rows // 64 if rows % 64 == 0 else 1
    wide = jnp.bfloat16
    dma = pltpu.SemaphoreType.DMA
    return pl.pallas_call(
        functools.partial(kernel, groups, stretches, count, pack, rows, fine, sub),
        out_shape=pltpu.VMEM((rows, width), wide),
        in_specs=[pl.BlockSpec(memory_space=pltpu.SMEM)] * 2
        + [pl.BlockSpec(memory_space=pltpu.HBM)] * 3,
        out_specs=pl.BlockSpec(memory_space=pltpu.VMEM),
        scratch_shapes=[
            pltpu.VMEM((count, span, unit), wide),
            pltpu.VMEM((count, span + tail, unit), wide),
            pltpu.VMEM((count, span + tail, unit), wide),
            pltpu.VMEM((count, tail, unit), wide),
            pltpu.VMEM((count, tail, unit), wide),
            pltpu.VMEM((count, span, unit), wide),
            pltpu.VMEM((1, span + tail), jnp.float32),
            dma((2, count, groups - 1)),
            dma((2, count, groups - 1)),
            dma((3, count)),
            dma((count, groups - 1, fine)),
            dma((count, groups - 1, fine)),
            dma((count, groups - 1, fine)),
            dma((count, groups - 1, fine)),
            dma((count,)),
            dma((2, count)),
            dma((2, count)),
        ],
        compiler_params=pltpu.CompilerParams(
            collective_id=0, has_side_effects=True, vmem_limit_bytes=58 * 1024 * 1024
        ),
        cost_estimate=pl.CostEstimate(
            flops=4 * span * (span + tail) * local,
            bytes_accessed=8 * rows * width,
            transcendentals=span * (span + tail) * heads,
        ),
    )(frames, motion, queries, keys, values)


def solution(mesh):
    placed = P(("cfg", "stretch", "head"), None)
    return jax.shard_map(
        functools.partial(body, mesh.shape["head"], mesh.shape["stretch"]),
        mesh=mesh,
        in_specs=(placed, placed, placed, P(), P()),
        out_specs=placed,
        check_vma=False,
    )
```

```python
import functools
import math

import jax
import jax.numpy as jnp
from jax import lax
from jax.experimental import pallas as pl
from jax.experimental.pallas import tpu as pltpu
from jax.sharding import PartitionSpec as P

HD = 128
FT = 128
FRAMES = 7
MOT_CAP = 4
NEG = -1e30
MESH = pl.DeviceIdType.MESH

PACK = 4
AHEAD = 3
LEAD = 2
LAG = 1


def kernel(
    groups, stretches, count, pack, rows, fine, sub,
    frames_ref, motion_ref, q_ref, k_ref, v_ref, out_ref,
    qb, kb, vb, kt, vt, ob, bias,
    in_send, in_recv, in_local, q_send, q_recv, out_send, out_recv, out_local, mot_send, mot_recv,
):
    span = rows * groups
    tail = MOT_CAP * FT
    unit = pack * HD
    local = count * unit
    me = lax.axis_index("head")
    stretch = lax.axis_index("stretch")
    has_after = stretch < stretches - 1
    has_before = stretch > 0
    after = jnp.minimum(stretch + 1, stretches - 1)
    before = jnp.maximum(stretch - 1, 0)
    live_frames = frames_ref[stretch]
    motion_frames = motion_ref[stretch]

    def peer(offset):
        return lax.rem(me + offset, groups)

    def columns(owner, index):
        return pl.ds(pl.multiple_of(owner * local + index * unit, unit), unit)

    def part_rows(base, part, parts):
        size = rows // parts
        return pl.ds(pl.multiple_of(base + part * size, 16), size)

    sources = (k_ref, v_ref, q_ref)
    targets = (kb, vb, qb)

    def exchange(which, index, offset, owner):
        to = peer(offset)
        land = me if owner is None else owner
        return pltpu.make_async_remote_copy(
            src_ref=sources[which].at[:, columns(to, index)],
            dst_ref=targets[which].at[index, part_rows(land * rows, 0, 1), :],
            send_sem=in_send.at[which, index, offset - 1],
            recv_sem=in_recv.at[which, index, offset - 1],
            device_id={"head": to},
            device_id_type=MESH,
        )

    def query(index, offset, owner, part, parts):
        to = peer(offset)
        land = me if owner is None else owner
        return pltpu.make_async_remote_copy(
            src_ref=q_ref.at[part_rows(0, part, parts), columns(to, index)],
            dst_ref=qb.at[index, part_rows(land * rows, part, parts), :],
            send_sem=q_send.at[index, offset - 1, part],
            recv_sem=q_recv.at[index, offset - 1, part],
            device_id={"head": to},
            device_id_type=MESH,
        )

    def keep(which, index):
        return pltpu.make_async_copy(
            sources[which].at[:, columns(me, index)],
            targets[which].at[index, part_rows(me * rows, 0, 1), :],
            in_local.at[which, index],
        )

    def pass_on(which, index):
        return pltpu.make_async_remote_copy(
            src_ref=(kt, vt)[which].at[index],
            dst_ref=(kb, vb)[which].at[index, pl.ds(span, tail), :],
            send_sem=mot_send.at[which, index],
            recv_sem=mot_recv.at[which, index],
            device_id={"stretch": after},
            device_id_type=MESH,
        )

    def give_back(index, offset, owner, part, parts):
        to = peer(offset)
        group = me if owner is None else owner
        return pltpu.make_async_remote_copy(
            src_ref=ob.at[index, part_rows(to * rows, part, parts), :],
            dst_ref=out_ref.at[part_rows(0, part, parts), columns(group, index)],
            send_sem=out_send.at[index, offset - 1, part],
            recv_sem=out_recv.at[index, offset - 1, part],
            device_id={"head": to},
            device_id_type=MESH,
        )

    def own_output(index):
        return pltpu.make_async_copy(
            ob.at[index, part_rows(me * rows, 0, 1), :],
            out_ref.at[:, columns(me, index)],
            out_local.at[index],
        )

    def send_queries(index, parts):
        for part in range(parts):
            for offset in range(1, groups):
                query(index, offset, None, part, parts).start()
        keep(2, index).start()

    def slot(index):
        @pl.when(index < count)
        def _():
            for which in range(2):
                for offset in range(1, groups):
                    exchange(which, index, offset, None).start()
                keep(which, index).start()

        @pl.when(jnp.logical_and(index >= LEAD, index < count + LEAD - 1))
        def _():
            send_queries(index - LEAD, 1)

        @pl.when(index == count + LEAD - 1)
        def _():
            send_queries(count - 1, fine)

    def forward(index):
        for which, (buffer, ready) in enumerate(((kb, kt), (vb, vt))):
            keep(which, index).wait()
            for offset in range(1, groups):
                exchange(which, index, offset, peer(groups - offset)).wait_recv()
            for block in range(MOT_CAP):
                chosen = buffer[index, pl.ds(block * FT, FT), :].astype(jnp.float32)
                for skip in range(1, FRAMES - MOT_CAP + 1):
                    other = buffer[index, pl.ds((block + skip) * FT, FT), :].astype(jnp.float32)
                    chosen = jnp.where(live_frames == MOT_CAP + skip, other, chosen)
                ready[index, pl.ds(block * FT, FT), :] = chosen.astype(jnp.bfloat16)

            @pl.when(has_after)
            def _():
                pass_on(which, index).start()

    scale = math.log2(math.e) / math.sqrt(HD)

    def attend(index, base, size):
        row = base + lax.broadcasted_iota(jnp.int32, (size, 1), 0)
        for head in range(pack):
            lanes = slice(head * HD, (head + 1) * HD)
            scores = lax.dot_general(
                qb[index, pl.ds(base, size), lanes], kb[index, :, lanes],
                (((1,), (1,)), ((), ())), preferred_element_type=jnp.float32,
            )
            scores = scores * scale + bias[...]
            top = jnp.max(scores, axis=1, keepdims=True)
            weights = jnp.exp2(scores - top)
            total = jnp.sum(weights, axis=1, keepdims=True)
            acc = jnp.dot(
                weights.astype(jnp.bfloat16), vb[index, :, lanes],
                preferred_element_type=jnp.float32,
            )
            mixed = jnp.where(row < live_frames * FT, acc / total, 0.0)
            ob[index, pl.ds(base, size), lanes] = mixed.astype(jnp.bfloat16)

    def attend_rows(index, begin, number):
        size = min(sub, number)

        def block(step, carry):
            attend(index, pl.multiple_of(begin + step * size, 16), size)
            return carry

        lax.fori_loop(0, number // size, block, 0)

    barrier = pltpu.get_barrier_semaphore()
    for offset in range(1, groups):
        pl.semaphore_signal(barrier, inc=1, device_id={"head": peer(offset)}, device_id_type=MESH)
    for other, there in ((after, has_after), (before, has_before)):

        @pl.when(there)
        def _():
            pl.semaphore_signal(barrier, inc=1, device_id={"stretch": other}, device_id_type=MESH)

    pl.semaphore_wait(
        barrier, groups - 1 + has_after.astype(jnp.int32) + has_before.astype(jnp.int32)
    )

    for index in range(AHEAD):
        slot(jnp.int32(index))

    spot = lax.broadcasted_iota(jnp.int32, (1, span + tail), 1)
    own = jnp.logical_and(spot < span, spot < live_frames * FT)
    mot = spot >= span + (MOT_CAP - motion_frames) * FT
    bias[...] = jnp.where(jnp.logical_or(own, mot), 0.0, NEG)

    @pl.when(jnp.logical_not(has_before))
    def _():
        def clear(index, carry):
            for buffer in (kb, vb):
                buffer[index, pl.ds(span, tail), :] = jnp.zeros((tail, unit), jnp.bfloat16)
            return carry

        lax.fori_loop(0, count, clear, 0)

    for index in range(LEAD):
        forward(jnp.int32(index))

    def work(index, parts):
        slot(index + AHEAD)

        @pl.when(index + LEAD < count)
        def _():
            forward(index + LEAD)

        @pl.when(has_before)
        def _():
            for which in range(2):
                pass_on(which, index).wait_recv()

        keep(2, index).wait()
        attend_rows(index, me * rows, rows)
        own_output(index).start()
        for offset in range(1, groups):
            to = peer(offset)

            def chunk(part, carry):
                query(index, groups - offset, to, part, parts).wait_recv()
                attend_rows(index, to * rows + part * (rows // parts), rows // parts)
                give_back(index, offset, None, part, parts).start()
                return carry

            lax.fori_loop(0, parts, chunk, 0)

    def retire(index, parts):
        for offset in range(1, groups):
            for which in range(2):
                exchange(which, index, offset, None).wait_send()
            for part in range(parts):
                query(index, offset, None, part, parts).wait_send()
                give_back(index, offset, None, part, parts).wait_send()
                give_back(index, offset, peer(groups - offset), part, parts).wait_recv()

        @pl.when(has_after)
        def _():
            for which in range(2):
                pass_on(which, index).wait_send()

        own_output(index).wait()

    def step(index, carry):
        work(index, 1)

        @pl.when(index >= LAG)
        def _():
            retire(index - LAG, 1)

        return carry

    lax.fori_loop(0, count - 1, step, 0)
    work(jnp.int32(count - 1), fine)
    for index in range(max(count - 1 - LAG, 0), count - 1):
        retire(jnp.int32(index), 1)
    retire(jnp.int32(count - 1), fine)


def store(pieces, held, out_ref, sems):
    size = held.shape[0] // pieces

    def piece(index):
        part = pl.ds(index * size, size)
        return pltpu.make_async_copy(held.at[part, :], out_ref.at[part, :], sems.at[index])

    for index in range(pieces):
        piece(index).start()
    for index in range(pieces):
        piece(index).wait()


def body(groups, stretches, queries, keys, values, frames, motion):
    rows, width = queries.shape
    span = rows * groups
    tail = MOT_CAP * FT
    local = width // groups
    heads = local // HD
    pack = math.gcd(heads, PACK)
    count = heads // pack
    unit = pack * HD
    sub = rows // 2 if rows % 64 == 0 else rows
    fine = rows // 64 if rows % 64 == 0 else 1
    pieces = 7
    wide = jnp.bfloat16
    dma = pltpu.SemaphoreType.DMA
    result = pl.pallas_call(
        functools.partial(kernel, groups, stretches, count, pack, rows, fine, sub),
        out_shape=pltpu.VMEM((rows, width), wide),
        in_specs=[pl.BlockSpec(memory_space=pltpu.SMEM)] * 2
        + [pl.BlockSpec(memory_space=pltpu.HBM)] * 3,
        out_specs=pl.BlockSpec(memory_space=pltpu.VMEM),
        scratch_shapes=[
            pltpu.VMEM((count, span, unit), wide),
            pltpu.VMEM((count, span + tail, unit), wide),
            pltpu.VMEM((count, span + tail, unit), wide),
            pltpu.VMEM((count, tail, unit), wide),
            pltpu.VMEM((count, tail, unit), wide),
            pltpu.VMEM((count, span, unit), wide),
            pltpu.VMEM((1, span + tail), jnp.float32),
            dma((2, count, groups - 1)),
            dma((2, count, groups - 1)),
            dma((3, count)),
            dma((count, groups - 1, fine)),
            dma((count, groups - 1, fine)),
            dma((count, groups - 1, fine)),
            dma((count, groups - 1, fine)),
            dma((count,)),
            dma((2, count)),
            dma((2, count)),
        ],
        compiler_params=pltpu.CompilerParams(
            collective_id=0, has_side_effects=True, vmem_limit_bytes=58 * 1024 * 1024
        ),
        cost_estimate=pl.CostEstimate(
            flops=4 * span * (span + tail) * local,
            bytes_accessed=8 * rows * width,
            transcendentals=span * (span + tail) * heads,
        ),
    )(frames, motion, queries, keys, values)
    return pl.pallas_call(
        functools.partial(store, pieces),
        out_shape=jax.ShapeDtypeStruct((rows, width), wide),
        in_specs=[pl.BlockSpec(memory_space=pltpu.VMEM)],
        out_specs=pl.BlockSpec(memory_space=pltpu.HBM),
        scratch_shapes=[dma((pieces,))],
        compiler_params=pltpu.CompilerParams(vmem_limit_bytes=16 * 1024 * 1024),
        cost_estimate=pl.CostEstimate(
            flops=0, bytes_accessed=4 * rows * width, transcendentals=0
        ),
    )(result)


def solution(mesh):
    placed = P(("cfg", "stretch", "head"), None)
    return jax.shard_map(
        functools.partial(body, mesh.shape["head"], mesh.shape["stretch"]),
        mesh=mesh,
        in_specs=(placed, placed, placed, P(), P()),
        out_specs=placed,
        check_vma=False,
    )
```
